32 devices in a mesh: dp: 4 (over z), seq: 2 (over y), tensor: 4 (over x, core).
Axes of the slice: x: 2, y: 2, z: 4, core: 2. Of those that a mesh axis runs over, the one named last changes fastest.
Arguments:
- tokens: bfloat16 [8, 1024, 1152], P('dp', 'seq'), may hold values from -6 to 6
- positions: int32 [8, 1024], P('dp', 'seq'), may hold values from 0 to 2046, as said below
- out_grad: bfloat16 [8, 1024, 1152], P('dp', 'seq'), may hold values from -6 to 6
- q_weight: bfloat16 [1152, 1024], P(('dp', 'seq'), 'tensor'), may hold values from -0.1875 to 0.1875
- kv_weight: bfloat16 [1152, 512], P(('dp', 'seq', 'tensor')), may hold values from -0.1875 to 0.1875
- o_weight: bfloat16 [1024, 1152], P('tensor', ('dp', 'seq')), may hold values from -0.1875 to 0.1875
- gate_weight: bfloat16 [1152, 6912], P(('dp', 'seq'), 'tensor'), may hold values from -0.1875 to 0.1875
- up_weight: bfloat16 [1152, 6912], P(('dp', 'seq'), 'tensor'), may hold values from -0.1875 to 0.1875
- down_weight: bfloat16 [6912, 1152], P('tensor', ('dp', 'seq')), may hold values from -0.078125 to 0.078125
- attn_in_gain: bfloat16 [1152], P(('dp', 'seq', 'tensor')), may hold values from -0.5 to 0.5
- attn_out_gain: bfloat16 [1152], P(('dp', 'seq', 'tensor')), may hold values from -0.5 to 0.5
- ffn_in_gain: bfloat16 [1152], P(('dp', 'seq', 'tensor')), may hold values from -0.5 to 0.5
- ffn_out_gain: bfloat16 [1152], P(('dp', 'seq', 'tensor')), may hold values from -0.5 to 0.5
- q_gain: bfloat16 [256], P(('dp', 'seq', 'tensor')), may hold values from -0.5 to 0.5
- k_gain: bfloat16 [256], P(('dp', 'seq', 'tensor')), may hold values from -0.5 to 0.5
Outputs:
- result: bfloat16 [8, 1024, 1152], P('dp', 'seq')
- input_grad: bfloat16 [8, 1024, 1152], P('dp', 'seq')
- q_weight_grad: float32 [1152, 1024], P(('dp', 'seq'), 'tensor')
- kv_weight_grad: float32 [1152, 512], P(('dp', 'seq', 'tensor'))
- o_weight_grad: float32 [1024, 1152], P('tensor', ('dp', 'seq'))
- gate_weight_grad: float32 [1152, 6912], P(('dp', 'seq'), 'tensor')
- up_weight_grad: float32 [1152, 6912], P(('dp', 'seq'), 'tensor')
- down_weight_grad: float32 [6912, 1152], P('tensor', ('dp', 'seq'))
- attn_in_gain_grad: float32 [1152], P(('dp', 'seq', 'tensor'))
- attn_out_gain_grad: float32 [1152], P(('dp', 'seq', 'tensor'))
- ffn_in_gain_grad: float32 [1152], P(('dp', 'seq', 'tensor'))
- ffn_out_gain_grad: float32 [1152], P(('dp', 'seq', 'tensor'))
- q_gain_grad: float32 [256], P(('dp', 'seq', 'tensor'))
- k_gain_grad: float32 [256], P(('dp', 'seq', 'tensor'))
The draws below stay inside these ranges and needn't reach their ends.
Inputs may be any that keep to these rules, and one draw needn't show every extreme that they name: `positions`: in every sequence the token of index i has position 2 i or 2 i - 1; the first token has 0 and the last 2 (1023).
All inputs are finite; a program needn't handle non-finite values.
Results may differ from the reference program's by a relative error of at most 0.025.
Values may be sent and summed in bfloat16 or wider, within the bound.
A program may use at most 192 MiB of HBM per device.

```python
import jax
import jax.numpy as jnp
from jax import lax

D = 1152
HEADS = 4
HEAD = 256
FF = 6912
LEN = 1024
SEQS = 8


def draw_positions(key, part):
    key = jax.random.fold_in(key, 7)
    lowered = jax.random.randint(key, (SEQS, LEN), 0, 2)
    index_v = jnp.arange(LEN, dtype=jnp.int32)
    edge_v = (index_v == 0) | (index_v == LEN - 1)
    lowered = jnp.where(edge_v[None, :], 0, lowered)
    return (2 * index_v[None, :] - lowered).astype(jnp.int32)


def block_levels(stream_key, extent, cuts, smallest, largest):
    def one(axis_at, parts):
        steps = jax.random.uniform(jax.random.fold_in(jax.random.fold_in(stream_key, 6), axis_at), (parts,), jnp.float32, smallest / len(cuts), largest / len(cuts))
        return jnp.repeat(jnp.exp(steps), extent[axis_at] // parts).reshape((-1,) + (1,) * (len(extent) - axis_at - 1))

    gain = one(*cuts[0])
    for cut in cuts[1:]:
        gain = gain * one(*cut)
    return gain


def centred(key, dims, spread, most, shards=(), kind=jnp.bfloat16):
    values = spread * jax.random.normal(key, dims, jnp.float32)
    if shards:
        values = values * block_levels(key, dims, shards, -0.22, 0.18)
    return jnp.clip(values, -most, most).astype(kind)


def setup_inputs(seed: int = 0) -> dict:
    key_of = jax.random.split(jax.random.key(seed), 16)
    tokens = centred(key_of[0], (SEQS, LEN, D), 1.0, 6.0, ((0, 4), (1, 2)))
    positions = draw_positions(jax.random.fold_in(key_of[15], 71), 0)
    out_grad = centred(key_of[2], (SEQS, LEN, D), 1.0, 6.0, ((0, 4), (1, 2)))
    q_weight = centred(key_of[3], (D, HEADS * HEAD), D ** -0.5, 0.1875, ((0, 8), (1, 4)))
    kv_weight = centred(key_of[4], (D, 2 * HEAD), D ** -0.5, 0.1875, ((0, 32),))
    o_weight = centred(key_of[5], (HEADS * HEAD, D), (HEADS * HEAD) ** -0.5, 0.1875, ((0, 4), (1, 8)))
    gate_weight = centred(key_of[6], (D, FF), D ** -0.5, 0.1875, ((0, 8), (1, 4)))
    up_weight = centred(key_of[7], (D, FF), D ** -0.5, 0.1875, ((0, 8), (1, 4)))
    down_weight = centred(key_of[8], (FF, D), FF ** -0.5, 0.078125, ((0, 4), (1, 8)))
    attn_in_gain = jnp.clip(jax.random.uniform(key_of[9], (D,), jnp.float32, -0.5, 0.5) * block_levels(key_of[9], (D,), ((0, 32),), -0.4, 0.0), -0.5, 0.5).astype(jnp.bfloat16)
    attn_out_gain = jnp.clip(jax.random.uniform(key_of[10], (D,), jnp.float32, -0.5, 0.5) * block_levels(key_of[10], (D,), ((0, 32),), -0.4, 0.0), -0.5, 0.5).astype(jnp.bfloat16)
    ffn_in_gain = jnp.clip(jax.random.uniform(key_of[11], (D,), jnp.float32, -0.5, 0.5) * block_levels(key_of[11], (D,), ((0, 32),), -0.4, 0.0), -0.5, 0.5).astype(jnp.bfloat16)
    ffn_out_gain = jnp.clip(jax.random.uniform(key_of[12], (D,), jnp.float32, -0.5, 0.5) * block_levels(key_of[12], (D,), ((0, 32),), -0.4, 0.0), -0.5, 0.5).astype(jnp.bfloat16)
    q_gain = jnp.clip(jax.random.uniform(key_of[13], (HEAD,), jnp.float32, -0.5, 0.5) * block_levels(key_of[13], (HEAD,), ((0, 32),), -0.4, 0.0), -0.5, 0.5).astype(jnp.bfloat16)
    k_gain = jnp.clip(jax.random.uniform(key_of[14], (HEAD,), jnp.float32, -0.5, 0.5) * block_levels(key_of[14], (HEAD,), ((0, 32),), -0.4, 0.0), -0.5, 0.5).astype(jnp.bfloat16)
    return dict(tokens=tokens, positions=positions, out_grad=out_grad, q_weight=q_weight, kv_weight=kv_weight, o_weight=o_weight, gate_weight=gate_weight, up_weight=up_weight, down_weight=down_weight, attn_in_gain=attn_in_gain, attn_out_gain=attn_out_gain, ffn_in_gain=ffn_in_gain, ffn_out_gain=ffn_out_gain, q_gain=q_gain, k_gain=k_gain)


@jax.custom_vjp
def low(v):
    return lax.optimization_barrier(v.astype(jnp.bfloat16)).astype(jnp.float32)

@jax.custom_vjp
def low_back(v):
    return v

def low_keep(v):
    return (low(v), None)

def low_pass(kept, grad):
    return (grad,)

def back_keep(v):
    return (v, None)

def back_low(kept, grad):
    return (low(grad),)
low.defvjp(low_keep, low_pass)
low_back.defvjp(back_keep, back_low)
EPS = 1e-06
QSCALE = 0.0625
MASKED = -1e+30
HIGH = lax.Precision.HIGHEST

def rms_norm(values):
    return values * lax.rsqrt(lax.optimization_barrier(jnp.mean(values * values, axis=-1, keepdims=True)) + EPS)

def angles(positions, width_n):
    half_w = width_n // 2
    freq_t = 1000000.0 ** (-(jnp.arange(half_w, dtype=jnp.float32) * 2.0 / width_n))
    turn_t = positions.astype(jnp.float32)[..., None] * freq_t
    turn_t = jnp.concatenate([turn_t, turn_t], axis=-1)
    return (jnp.cos(turn_t), jnp.sin(turn_t))

def rotate(values, cos_t, sin_t):
    half_w = values.shape[-1] // 2
    turned = jnp.concatenate([-values[..., half_w:], values[..., :half_w]], axis=-1)
    return values * cos_t + turned * sin_t

def matmul(left_m, right_m):
    return jnp.dot(left_m, right_m, precision=HIGH, preferred_element_type=jnp.float32)

def layer_fn(inputs, positions, params):
    q_mat, kv_mat, o_mat, gate_mat, up_mat, down_mat, gain_ai, gain_ao, gain_fi, gain_fo, gain_q, gain_k = params
    length = inputs.shape[0]
    normed = low(rms_norm(inputs) * (1.0 + gain_ai))
    q_raw = low_back(matmul(normed, q_mat)).reshape(length, HEADS, HEAD).transpose(1, 0, 2)
    kv_raw = matmul(normed, kv_mat)
    kv_heads = low_back(jnp.broadcast_to(kv_raw[None], (HEADS, length, 2 * HEAD)))
    cos_t, sin_t = angles(positions, HEAD)
    queries = low(rotate(rms_norm(q_raw) * (1.0 + gain_q), cos_t, sin_t) * QSCALE)
    keys = low(rotate(rms_norm(kv_heads[..., :HEAD]) * (1.0 + gain_k), cos_t, sin_t))
    values = low(kv_heads[..., HEAD:])
    scores = jnp.einsum('hqd,hkd->hqk', queries, keys, precision=HIGH)
    causal = jnp.arange(length)[:, None] >= jnp.arange(length)[None, :]
    scores = low_back(jnp.where(causal[None], scores, MASKED))
    probs = low(jax.nn.softmax(scores, axis=-1))
    attended = low(low_back(jnp.einsum('hqk,hkd->hqd', probs, values, precision=HIGH)))
    attended = attended.transpose(1, 0, 2).reshape(length, HEADS * HEAD)
    branch = low_back(matmul(attended, o_mat))
    middle = inputs + rms_norm(branch) * (1.0 + gain_ao)
    normed_ffn = low(rms_norm(middle) * (1.0 + gain_fi))
    gate_v = low_back(matmul(normed_ffn, gate_mat))
    upper_v = low_back(matmul(normed_ffn, up_mat))
    acted = low(jax.nn.gelu(gate_v, approximate=True) * upper_v)
    ffn_out = low_back(matmul(acted, down_mat))
    return middle + rms_norm(ffn_out) * (1.0 + gain_fo)

def reference(tokens, positions, out_grad, q_weight, kv_weight, o_weight, gate_weight, up_weight, down_weight, attn_in_gain, attn_out_gain, ffn_in_gain, ffn_out_gain, q_gain, k_gain):
    params = tuple((entry.astype(jnp.float32) for entry in (q_weight, kv_weight, o_weight, gate_weight, up_weight, down_weight, attn_in_gain, attn_out_gain, ffn_in_gain, ffn_out_gain, q_gain, k_gain)))

    def one_seq(totals, item):
        seq_tokens, seq_positions, seq_grad = item

        def forward_fn(inputs, weights):
            return layer_fn(inputs, seq_positions, weights)
        output, pull_back = jax.vjp(forward_fn, seq_tokens.astype(jnp.float32), params)
        d_input, d_params = pull_back(seq_grad.astype(jnp.float32))
        totals = jax.tree.map(jnp.add, totals, d_params)
        return (totals, (output.astype(jnp.bfloat16), d_input.astype(jnp.bfloat16)))
    zero_set = tuple((jnp.zeros(entry.shape, jnp.float32) for entry in params))
    totals, (outputs, d_inputs) = lax.scan(one_seq, zero_set, (tokens, positions, out_grad))
    return (outputs, d_inputs, totals[0], totals[1], totals[2], totals[3], totals[4], totals[5], totals[6], totals[7], totals[8], totals[9], totals[10], totals[11])
```

```python
import jax
import jax.numpy as jnp
from jax import lax
from jax.sharding import PartitionSpec as P

EPS = 1e-06
QSCALE = 0.0625
MASKED = -1e30
LOW = jnp.bfloat16
F32 = jnp.float32
ALL = ("dp", "seq", "tensor")


def normalize(values):
    factor = lax.rsqrt(jnp.mean(values * values, axis=-1, keepdims=True) + EPS)
    return (values * factor, factor)


def norm_back(scaled, factor, upstream):
    return factor * (upstream - scaled * jnp.mean(upstream * scaled, axis=-1, keepdims=True))


def angles(positions, width_n):
    half_w = width_n // 2
    freq_t = 1000000.0 ** (-(jnp.arange(half_w, dtype=F32) * 2.0 / width_n))
    turn_t = positions.astype(F32)[..., None] * freq_t
    return (jnp.cos(turn_t), jnp.sin(turn_t))


def rotate(values, cos_t, sin_t):
    half_w = values.shape[-1] // 2
    low_v, high_v = values[..., :half_w], values[..., half_w:]
    return jnp.concatenate(
        [low_v * cos_t - high_v * sin_t, high_v * cos_t + low_v * sin_t], axis=-1
    )


def rotate_back(values, cos_t, sin_t):
    half_w = values.shape[-1] // 2
    low_v, high_v = values[..., :half_w], values[..., half_w:]
    return jnp.concatenate(
        [low_v * cos_t + high_v * sin_t, high_v * cos_t - low_v * sin_t], axis=-1
    )


def product(pattern, left_m, right_m):
    return jnp.einsum(pattern, left_m, right_m, preferred_element_type=F32)


def gelu_mix(gate_v, upper_v):
    return jax.nn.gelu(gate_v, approximate=True) * upper_v


def swap(values):
    return lax.ppermute(values, "seq", [(0, 1), (1, 0)])


def in_order(mine, theirs, axis):
    first = lax.axis_index("seq") == 0
    return jnp.stack(
        [jnp.where(first, mine, theirs), jnp.where(first, theirs, mine)], axis=axis
    )


def gather_rows(shard):
    seq_n = lax.axis_size("seq")
    if seq_n != 2:
        return lax.all_gather(shard, ("dp", "seq"), axis=0, tiled=True)
    mine = lax.all_gather(shard, "dp", axis=0, tiled=False)
    both = in_order(mine, swap(mine), 1)
    return both.reshape(-1, shard.shape[-1])


def scatter_rows(total):
    seq_n = lax.axis_size("seq")
    total = total.astype(LOW)
    if seq_n != 2:
        return lax.psum_scatter(
            total, ("dp", "seq"), scatter_dimension=0, tiled=True
        ).astype(F32)
    dp_n = lax.axis_size("dp")
    me = lax.axis_index("seq")
    parts = total.reshape(dp_n, 2, -1, total.shape[-1])
    away = lax.dynamic_index_in_dim(parts, 1 - me, 1, keepdims=False)
    stay = lax.dynamic_index_in_dim(parts, me, 1, keepdims=False)
    pair = (stay.astype(F32) + swap(away).astype(F32)).astype(LOW)
    pair = pair.reshape(-1, total.shape[-1])
    return lax.psum_scatter(pair, "dp", scatter_dimension=0, tiled=True).astype(F32)


def sum_share(partial):
    return lax.psum_scatter(
        partial.astype(LOW), "tensor", scatter_dimension=0, tiled=True
    ).astype(F32)


def spread(share):
    return lax.all_gather(share, "tensor", axis=0, tiled=True)


def row_sum(values):
    return jnp.sum(values.reshape(-1, values.shape[-1]), axis=0)


def body(
    tokens,
    positions,
    out_grad,
    q_weight,
    kv_weight,
    o_weight,
    gate_weight,
    up_weight,
    down_weight,
    attn_in_gain,
    attn_out_gain,
    ffn_in_gain,
    ffn_out_gain,
    q_gain,
    k_gain,
):
    batch, local_len, width = tokens.shape
    rows_n = batch * local_len
    head = q_weight.shape[1]
    seq_n, tensor_n = lax.axis_size("seq"), lax.axis_size("tensor")
    blocks_n = lax.axis_size("dp") * seq_n
    all_n = blocks_n * tensor_n
    part = width // all_n
    head_part = head // all_n
    share_n = rows_n // tensor_n
    tensor_me = lax.axis_index("tensor")

    gain_row = jnp.concatenate(
        [attn_in_gain, attn_out_gain, ffn_in_gain, ffn_out_gain, q_gain, k_gain]
    )
    gain_n = gain_row.shape[0]
    gain_row = jnp.pad(gain_row, (0, 2 * head - gain_n))[None]
    small = lax.all_gather(
        jnp.concatenate([kv_weight, gain_row], axis=0), ALL, axis=0, tiled=False
    )
    kv_mat = small[:, :part].reshape(width, 2 * head)
    gains = small[:, part, :gain_n].astype(F32)

    def gain_of(index):
        return 1.0 + gains[:, index * part : (index + 1) * part].reshape(width)

    scale_ai, scale_ao, scale_fi, scale_fo = (gain_of(index) for index in range(4))
    tail = 4 * part
    scale_q = 1.0 + gains[:, tail : tail + head_part].reshape(head)
    scale_k = 1.0 + gains[:, tail + head_part :].reshape(head)

    qo_mat = gather_rows(jnp.concatenate([q_weight, o_weight.T], axis=1))
    q_mat, o_mat = qo_mat[:, :head], qo_mat[:, head:]
    gate_mat = gather_rows(gate_weight)
    up_mat = gather_rows(up_weight)
    down_mat = gather_rows(down_weight.T)

    def share(values):
        return lax.dynamic_slice_in_dim(
            values.reshape(rows_n, width), tensor_me * share_n, share_n, 0
        ).astype(F32)

    cos_t, sin_t = angles(positions, head)
    in_hat_all, unused_fac = normalize(tokens.astype(F32))
    normed = (in_hat_all * scale_ai).astype(LOW)
    kv_raw = product("scd,de->sce", normed, kv_mat)
    k_hat, k_fac = normalize(kv_raw[..., :head])
    keys_local = rotate(k_hat * scale_k, cos_t, sin_t).astype(LOW)
    both_local = jnp.concatenate([keys_local, kv_raw[..., head:].astype(LOW)], axis=-1)
    if seq_n == 2:
        key_value = in_order(both_local, swap(both_local), 1)
        key_value = key_value.reshape(batch, 2 * local_len, 2 * head)
    else:
        key_value = lax.all_gather(both_local, "seq", axis=1, tiled=True)
    key_all, value_all = key_value[..., :head], key_value[..., head:]
    q_raw = product("scd,de->sce", normed, q_mat)
    q_hat, q_fac = normalize(q_raw)
    queries = (rotate(q_hat * scale_q, cos_t, sin_t) * QSCALE).astype(LOW)
    row_ids = lax.axis_index("seq") * local_len + jnp.arange(local_len, dtype=jnp.int32)
    all_ids = jnp.arange(seq_n * local_len, dtype=jnp.int32)
    allowed = all_ids[None, :] <= row_ids[:, None]
    scores = jnp.where(allowed[None], product("sqd,skd->sqk", queries, key_all), MASKED)
    peak_v = jnp.max(scores, axis=-1, keepdims=True)
    expo_v = jnp.exp(scores - peak_v)
    probs = expo_v / jnp.sum(expo_v, axis=-1, keepdims=True)
    probs_low = probs.astype(LOW)
    attended = product("sqk,skd->sqd", probs_low, value_all).astype(LOW)
    attended_r = attended.reshape(rows_n, head)
    branch = sum_share(product("re,de->rd", attended_r, o_mat))

    inputs = share(tokens)
    in_hat, in_fac = normalize(inputs)
    back = share(out_grad)
    br_hat, br_fac = normalize(branch)
    middle = inputs + br_hat * scale_ao
    mid_hat, mid_fac = normalize(middle)
    normed_ffn = spread((mid_hat * scale_fi).astype(LOW))
    gate_v = product("rd,df->rf", normed_ffn, gate_mat)
    upper_v = product("rd,df->rf", normed_ffn, up_mat)
    acted = gelu_mix(gate_v, upper_v).astype(LOW)
    ffn_out = sum_share(product("rf,df->rd", acted, down_mat))
    ffn_hat, ffn_fac = normalize(ffn_out)
    g_fo = row_sum(back * ffn_hat)
    d_ffn = spread(norm_back(ffn_hat, ffn_fac, back * scale_fo).astype(LOW))
    result = spread((middle + ffn_hat * scale_fo).astype(LOW)).reshape(tokens.shape)

    g_down = scatter_rows(product("rd,rf->df", d_ffn, acted)).T
    d_acted = product("rd,df->rf", d_ffn, down_mat)
    unused_out, pull_back = jax.vjp(gelu_mix, gate_v, upper_v)
    d_gate, d_up = pull_back(d_acted)
    d_gate = d_gate.astype(LOW)
    d_up = d_up.astype(LOW)
    d_nffn = sum_share(
        product("rf,df->rd", d_gate, gate_mat) + product("rf,df->rd", d_up, up_mat)
    )
    g_gate = scatter_rows(product("rd,rf->df", normed_ffn, d_gate))
    g_up = scatter_rows(product("rd,rf->df", normed_ffn, d_up))
    g_fi = row_sum(d_nffn * mid_hat)
    d_middle = back + norm_back(mid_hat, mid_fac, d_nffn * scale_fi)
    g_ao = row_sum(d_middle * br_hat)
    d_branch = spread(norm_back(br_hat, br_fac, d_middle * scale_ao).astype(LOW))

    g_out = product("rd,re->de", d_branch, attended_r)
    d_att = product("rd,de->re", d_branch, o_mat).astype(LOW).reshape(attended.shape)
    d_probs = product("sqd,skd->sqk", d_att, value_all)
    row_dot = jnp.sum(probs * d_probs, axis=-1, keepdims=True)
    d_scores = (probs * (d_probs - row_dot)).astype(LOW)
    key_terms = product("sqk,sqd->skd", d_scores, queries)
    value_terms = product("sqk,sqd->skd", probs_low, d_att)
    kv_terms = jnp.concatenate([key_terms, value_terms], axis=-1).astype(LOW)
    if seq_n == 2:
        me = lax.axis_index("seq")
        halves = kv_terms.reshape(batch, 2, local_len, 2 * head)
        away = lax.dynamic_index_in_dim(halves, 1 - me, 1, keepdims=False)
        stay = lax.dynamic_index_in_dim(halves, me, 1, keepdims=False)
        d_kv = stay.astype(F32) + swap(away).astype(F32)
    else:
        d_kv = lax.psum_scatter(kv_terms, "seq", scatter_dimension=1, tiled=True).astype(F32)
    d_queries = product("sqk,skd->sqd", d_scores, key_all)
    dq_turn = rotate_back(d_queries * QSCALE, cos_t, sin_t)
    g_q = row_sum(dq_turn * q_hat)
    d_qraw = norm_back(q_hat, q_fac, dq_turn * scale_q).astype(LOW)
    dk_turn = rotate_back(d_kv[..., :head], cos_t, sin_t)
    g_k = row_sum(dk_turn * k_hat)
    d_kvraw = jnp.concatenate(
        [norm_back(k_hat, k_fac, dk_turn * scale_k), d_kv[..., head:]], axis=-1
    ).astype(LOW)
    d_normed = product("sce,de->scd", d_qraw, q_mat) + product("sce,de->scd", d_kvraw, kv_mat)
    d_normed = sum_share(d_normed.reshape(rows_n, width))
    g_kv = product("scd,sce->de", normed, d_kvraw).astype(LOW)
    g_kv = g_kv.reshape(blocks_n, tensor_n, part, 2 * head)
    g_kv = lax.psum_scatter(g_kv, "tensor", scatter_dimension=1, tiled=False)
    g_qmat = product("scd,sce->de", normed, d_qraw)
    g_qo = jnp.concatenate([g_qmat, g_out], axis=1).astype(LOW)
    g_qo = g_qo.reshape(blocks_n, width // blocks_n, 2 * head)
    fill = jnp.zeros((blocks_n, -(width // blocks_n + part) % 16, 2 * head), LOW)
    last = jnp.concatenate([g_qo, g_kv, fill], axis=1).reshape(-1, 2 * head)
    last = scatter_rows(last)
    own_n = width // blocks_n
    g_ai = row_sum(d_normed * in_hat)
    d_input = d_middle + norm_back(in_hat, in_fac, d_normed * scale_ai)
    d_input = spread(d_input.astype(LOW)).reshape(tokens.shape)
    gain_terms = jnp.concatenate(
        [entry.reshape(all_n, -1) for entry in (g_ai, g_ao, g_fi, g_fo, g_q, g_k)], axis=1
    )
    gain_sums = lax.psum_scatter(gain_terms, ALL, scatter_dimension=0, tiled=True)[0]
    return (
        result,
        d_input,
        last[:own_n, :head],
        last[own_n : own_n + part],
        last[:own_n, head:].T,
        g_gate,
        g_up,
        g_down,
        gain_sums[:part],
        gain_sums[part : 2 * part],
        gain_sums[2 * part : 3 * part],
        gain_sums[3 * part : 4 * part],
        gain_sums[tail : tail + head_part],
        gain_sums[tail + head_part :],
    )


def solution(mesh):
    in_specs = (
        P("dp", "seq", None),
        P("dp", "seq"),
        P("dp", "seq", None),
        P(("dp", "seq"), "tensor"),
        P(("dp", "seq", "tensor"), None),
        P("tensor", ("dp", "seq")),
        P(("dp", "seq"), "tensor"),
        P(("dp", "seq"), "tensor"),
        P("tensor", ("dp", "seq")),
        P(("dp", "seq", "tensor")),
        P(("dp", "seq", "tensor")),
        P(("dp", "seq", "tensor")),
        P(("dp", "seq", "tensor")),
        P(("dp", "seq", "tensor")),
        P(("dp", "seq", "tensor")),
    )
    out_specs = (
        P("dp", "seq", None),
        P("dp", "seq", None),
        P(("dp", "seq"), "tensor"),
        P(("dp", "seq", "tensor"), None),
        P("tensor", ("dp", "seq")),
        P(("dp", "seq"), "tensor"),
        P(("dp", "seq"), "tensor"),
        P("tensor", ("dp", "seq")),
        P(("dp", "seq", "tensor")),
        P(("dp", "seq", "tensor")),
        P(("dp", "seq", "tensor")),
        P(("dp", "seq", "tensor")),
        P(("dp", "seq", "tensor")),
        P(("dp", "seq", "tensor")),
    )
    return jax.shard_map(body, mesh=mesh, in_specs=in_specs, out_specs=out_specs, check_vma=False)
```

```python
import jax
import jax.numpy as jnp
from jax import lax
from jax.sharding import PartitionSpec as P

EPS = 1e-06
QSCALE = 0.0625
MASKED = -1e30
LOW = jnp.bfloat16
F32 = jnp.float32
ALL = ("dp", "seq", "tensor")


def normalize(values):
    factor = lax.rsqrt(jnp.mean(values * values, axis=-1, keepdims=True) + EPS)
    return (values * factor, factor)


def norm_back(scaled, factor, upstream):
    return factor * (upstream - scaled * jnp.mean(upstream * scaled, axis=-1, keepdims=True))


def angles(positions, width_n):
    half_w = width_n // 2
    freq_t = 1000000.0 ** (-(jnp.arange(half_w, dtype=F32) * 2.0 / width_n))
    turn_t = positions.astype(F32)[..., None] * freq_t
    return (jnp.cos(turn_t), jnp.sin(turn_t))


def rotate(values, cos_t, sin_t):
    half_w = values.shape[-1] // 2
    low_v, high_v = values[..., :half_w], values[..., half_w:]
    return jnp.concatenate(
        [low_v * cos_t - high_v * sin_t, high_v * cos_t + low_v * sin_t], axis=-1
    )


def rotate_back(values, cos_t, sin_t):
    half_w = values.shape[-1] // 2
    low_v, high_v = values[..., :half_w], values[..., half_w:]
    return jnp.concatenate(
        [low_v * cos_t + high_v * sin_t, high_v * cos_t - low_v * sin_t], axis=-1
    )


def product(pattern, left_m, right_m):
    return jnp.einsum(pattern, left_m, right_m, preferred_element_type=F32)


def gelu_mix(gate_v, upper_v):
    return jax.nn.gelu(gate_v, approximate=True) * upper_v


def swap(values):
    return lax.ppermute(values, "seq", [(0, 1), (1, 0)])


def in_order(mine, theirs, axis):
    first = lax.axis_index("seq") == 0
    return jnp.stack(
        [jnp.where(first, mine, theirs), jnp.where(first, theirs, mine)], axis=axis
    )


def gather_rows(shard):
    seq_n = lax.axis_size("seq")
    if seq_n != 2:
        return lax.all_gather(shard, ("dp", "seq"), axis=0, tiled=True)
    mine = lax.all_gather(shard, "dp", axis=0, tiled=False)
    both = in_order(mine, swap(mine), 1)
    return both.reshape(-1, shard.shape[-1])


def add_dp(pair):
    dp_n = lax.axis_size("dp")
    me = lax.axis_index("dp")
    total = lax.dynamic_index_in_dim(pair, me, 0, keepdims=False).astype(F32)
    for step in range(1, dp_n):
        sent = lax.dynamic_index_in_dim(pair, lax.rem(me + step, dp_n), 0, keepdims=False)
        total = total + lax.ppermute(
            sent, "dp", [(index, (index + step) % dp_n) for index in range(dp_n)]
        ).astype(F32)
    return total


def scatter_rows(total):
    seq_n = lax.axis_size("seq")
    if seq_n != 2:
        return lax.psum_scatter(
            total, ("dp", "seq"), scatter_dimension=0, tiled=True
        ).astype(F32)
    dp_n = lax.axis_size("dp")
    me = lax.axis_index("seq")
    parts = total.reshape(dp_n, 2, -1, total.shape[-1])
    away = lax.dynamic_index_in_dim(parts, 1 - me, 1, keepdims=False)
    stay = lax.dynamic_index_in_dim(parts, me, 1, keepdims=False)
    return add_dp((stay.astype(F32) + swap(away).astype(F32)).astype(LOW))


def across(values, bit):
    return lax.ppermute(values, "tensor", [(index, index ^ bit) for index in range(4)])


def add_tensor(parts):
    if lax.axis_size("tensor") != 4:
        return lax.psum_scatter(parts, "tensor", scatter_dimension=0).astype(F32)
    me = lax.axis_index("tensor")
    low, high = lax.rem(me, 2), me // 2
    pairs = parts.reshape((2, 2) + parts.shape[1:])
    sent = lax.dynamic_index_in_dim(pairs, 1 - low, 1, keepdims=False)
    kept = lax.dynamic_index_in_dim(pairs, low, 1, keepdims=False)
    kept = (kept.astype(F32) + across(sent, 1).astype(F32)).astype(LOW)
    sent = lax.dynamic_index_in_dim(kept, 1 - high, 0, keepdims=False)
    kept = lax.dynamic_index_in_dim(kept, high, 0, keepdims=False)
    return kept.astype(F32) + across(sent, 2).astype(F32)


def sum_share(partial):
    tensor_n = lax.axis_size("tensor")
    return add_tensor(partial.astype(LOW).reshape(tensor_n, -1, partial.shape[-1]))


def spread(share):
    if lax.axis_size("tensor") != 4:
        return lax.all_gather(share, "tensor", axis=0, tiled=True)
    me = lax.axis_index("tensor")
    even, first = lax.rem(me, 2) == 0, me // 2 == 0
    other = across(share, 2)
    both = jnp.stack([jnp.where(first, share, other), jnp.where(first, other, share)], axis=0)
    other = across(both, 1)
    full = jnp.stack([jnp.where(even, both, other), jnp.where(even, other, both)], axis=1)
    return full.reshape(-1, share.shape[-1])


def row_sum(values):
    return jnp.sum(values.reshape(-1, values.shape[-1]), axis=0)


def body(
    tokens,
    positions,
    out_grad,
    q_weight,
    kv_weight,
    o_weight,
    gate_weight,
    up_weight,
    down_weight,
    attn_in_gain,
    attn_out_gain,
    ffn_in_gain,
    ffn_out_gain,
    q_gain,
    k_gain,
):
    batch, local_len, width = tokens.shape
    rows_n = batch * local_len
    head = q_weight.shape[1]
    seq_n, tensor_n = lax.axis_size("seq"), lax.axis_size("tensor")
    blocks_n = lax.axis_size("dp") * seq_n
    all_n = blocks_n * tensor_n
    part = width // all_n
    head_part = head // all_n
    share_n = rows_n // tensor_n
    tensor_me = lax.axis_index("tensor")

    gain_row = jnp.concatenate(
        [attn_in_gain, attn_out_gain, ffn_in_gain, ffn_out_gain, q_gain, k_gain]
    )
    gain_n = gain_row.shape[0]
    gain_row = jnp.pad(gain_row, (0, 2 * head - gain_n))[None]
    fill = jnp.zeros((-(part + 1) % 16, 2 * head), LOW)
    small = lax.all_gather(
        jnp.concatenate([kv_weight, gain_row, fill], axis=0), ALL, axis=0, tiled=True
    ).reshape(all_n, -1, 2 * head)
    kv_mat = small[:, :part].reshape(width, 2 * head)
    gains = small[:, part, :gain_n].astype(F32)

    def gain_of(index):
        return 1.0 + gains[:, index * part : (index + 1) * part].reshape(width)

    scale_ai, scale_ao, scale_fi, scale_fo = (gain_of(index) for index in range(4))
    tail = 4 * part
    scale_q = 1.0 + gains[:, tail : tail + head_part].reshape(head)
    scale_k = 1.0 + gains[:, tail + head_part :].reshape(head)

    qo_mat = gather_rows(jnp.concatenate([q_weight, o_weight.T], axis=1))
    q_mat, o_mat = qo_mat[:, :head], qo_mat[:, head:]
    gate_mat = gather_rows(gate_weight)
    up_mat = gather_rows(up_weight)
    down_mat = gather_rows(down_weight.T)

    def share(values):
        return lax.dynamic_slice_in_dim(
            values.reshape(rows_n, width), tensor_me * share_n, share_n, 0
        ).astype(F32)

    cos_t, sin_t = angles(positions, head)
    in_hat_all, unused_fac = normalize(tokens.astype(F32))
    normed = (in_hat_all * scale_ai).astype(LOW)
    kv_raw = product("scd,de->sce", normed, kv_mat)
    k_hat, k_fac = normalize(kv_raw[..., :head])
    keys_local = rotate(k_hat * scale_k, cos_t, sin_t).astype(LOW)
    both_local = jnp.concatenate([keys_local, kv_raw[..., head:].astype(LOW)], axis=-1)
    if seq_n == 2:
        key_value = in_order(both_local, swap(both_local), 1)
        key_value = key_value.reshape(batch, 2 * local_len, 2 * head)
    else:
        key_value = lax.all_gather(both_local, "seq", axis=1, tiled=True)
    key_all, value_all = key_value[..., :head], key_value[..., head:]
    q_raw = product("scd,de->sce", normed, q_mat)
    q_hat, q_fac = normalize(q_raw)
    queries = (rotate(q_hat * scale_q, cos_t, sin_t) * QSCALE).astype(LOW)
    row_ids = lax.axis_index("seq") * local_len + jnp.arange(local_len, dtype=jnp.int32)
    all_ids = jnp.arange(seq_n * local_len, dtype=jnp.int32)
    allowed = all_ids[None, :] <= row_ids[:, None]
    scores = jnp.where(allowed[None], product("sqd,skd->sqk", queries, key_all), MASKED)
    peak_v = jnp.max(scores, axis=-1, keepdims=True)
    expo_v = jnp.exp(scores - peak_v)
    probs = expo_v / jnp.sum(expo_v, axis=-1, keepdims=True)
    probs_low = probs.astype(LOW)
    attended = product("sqk,skd->sqd", probs_low, value_all).astype(LOW)
    attended_r = attended.reshape(rows_n, head)
    branch = sum_share(product("re,de->rd", attended_r, o_mat))

    inputs = share(tokens)
    in_hat, in_fac = normalize(inputs)
    back = share(out_grad)
    br_hat, br_fac = normalize(branch)
    middle = inputs + br_hat * scale_ao
    mid_hat, mid_fac = normalize(middle)
    normed_ffn = spread((mid_hat * scale_fi).astype(LOW))
    gate_v = product("rd,df->rf", normed_ffn, gate_mat)
    upper_v = product("rd,df->rf", normed_ffn, up_mat)
    acted = gelu_mix(gate_v, upper_v).astype(LOW)
    ffn_out = sum_share(product("rf,df->rd", acted, down_mat))
    ffn_hat, ffn_fac = normalize(ffn_out)
    g_fo = row_sum(back * ffn_hat)
    d_ffn = spread(norm_back(ffn_hat, ffn_fac, back * scale_fo).astype(LOW))
    result = spread((middle + ffn_hat * scale_fo).astype(LOW)).reshape(tokens.shape)

    g_down = product("rd,rf->df", d_ffn, acted).astype(LOW)
    d_ffn, g_down = lax.optimization_barrier((d_ffn, g_down))
    g_down = scatter_rows(g_down).T
    d_acted = product("rd,df->rf", d_ffn, down_mat)
    unused_out, pull_back = jax.vjp(gelu_mix, gate_v, upper_v)
    d_gate, d_up = pull_back(d_acted)
    d_gate = d_gate.astype(LOW)
    d_up = d_up.astype(LOW)
    d_nffn = sum_share(
        product("rf,df->rd", d_gate, gate_mat) + product("rf,df->rd", d_up, up_mat)
    )
    g_gate = product("rd,rf->df", normed_ffn, d_gate).astype(LOW)
    g_up = product("rd,rf->df", normed_ffn, d_up).astype(LOW)
    d_nffn, g_gate, g_up = lax.optimization_barrier((d_nffn, g_gate, g_up))
    g_gate = scatter_rows(g_gate)
    g_up = scatter_rows(g_up)
    g_fi = row_sum(d_nffn * mid_hat)
    d_middle = back + norm_back(mid_hat, mid_fac, d_nffn * scale_fi)
    g_ao = row_sum(d_middle * br_hat)
    d_branch = spread(norm_back(br_hat, br_fac, d_middle * scale_ao).astype(LOW))

    g_out = product("rd,re->de", d_branch, attended_r)
    d_att = product("rd,de->re", d_branch, o_mat).astype(LOW).reshape(attended.shape)
    d_probs = product("sqd,skd->sqk", d_att, value_all)
    row_dot = jnp.sum(probs * d_probs, axis=-1, keepdims=True)
    d_scores = (probs * (d_probs - row_dot)).astype(LOW)
    key_terms = product("sqk,sqd->skd", d_scores, queries)
    value_terms = product("sqk,sqd->skd", probs_low, d_att)
    kv_terms = jnp.concatenate([key_terms, value_terms], axis=-1).astype(LOW)
    if seq_n == 2:
        me = lax.axis_index("seq")
        halves = kv_terms.reshape(batch, 2, local_len, 2 * head)
        away = lax.dynamic_index_in_dim(halves, 1 - me, 1, keepdims=False)
        stay = lax.dynamic_index_in_dim(halves, me, 1, keepdims=False)
        d_kv = stay.astype(F32) + swap(away).astype(F32)
    else:
        d_kv = lax.psum_scatter(kv_terms, "seq", scatter_dimension=1, tiled=True).astype(F32)
    d_queries = product("sqk,skd->sqd", d_scores, key_all)
    dq_turn = rotate_back(d_queries * QSCALE, cos_t, sin_t)
    g_q = row_sum(dq_turn * q_hat)
    d_qraw = norm_back(q_hat, q_fac, dq_turn * scale_q).astype(LOW)
    dk_turn = rotate_back(d_kv[..., :head], cos_t, sin_t)
    g_k = row_sum(dk_turn * k_hat)
    d_kvraw = jnp.concatenate(
        [norm_back(k_hat, k_fac, dk_turn * scale_k), d_kv[..., head:]], axis=-1
    ).astype(LOW)
    d_normed = product("sce,de->scd", d_qraw, q_mat) + product("sce,de->scd", d_kvraw, kv_mat)
    d_normed = sum_share(d_normed.reshape(rows_n, width))
    g_kv = product("scd,sce->de", normed, d_kvraw).astype(LOW)
    g_kv = g_kv.reshape(blocks_n, tensor_n, part, 2 * head)
    g_kv = add_tensor(jnp.swapaxes(g_kv, 0, 1).reshape(tensor_n, -1, 2 * head))
    g_kv = g_kv.astype(LOW).reshape(blocks_n, part, 2 * head)
    g_qmat = product("scd,sce->de", normed, d_qraw)
    g_qo = jnp.concatenate([g_qmat, g_out], axis=1).astype(LOW)
    g_qo = g_qo.reshape(blocks_n, width // blocks_n, 2 * head)
    fill = jnp.zeros((blocks_n, -(width // blocks_n + part) % 16, 2 * head), LOW)
    last = jnp.concatenate([g_qo, g_kv, fill], axis=1).reshape(-1, 2 * head)
    last = scatter_rows(last)
    own_n = width // blocks_n
    g_ai = row_sum(d_normed * in_hat)
    d_input = d_middle + norm_back(in_hat, in_fac, d_normed * scale_ai)
    d_input = spread(d_input.astype(LOW)).reshape(tokens.shape)
    gain_terms = jnp.concatenate(
        [entry.reshape(all_n, -1) for entry in (g_ai, g_ao, g_fi, g_fo, g_q, g_k)], axis=1
    )
    gain_all = lax.all_gather(gain_terms, ALL, axis=0, tiled=False)
    own = lax.dynamic_index_in_dim(gain_all, lax.axis_index(ALL), 1, keepdims=False)
    gain_sums = jnp.sum(own, axis=0)
    return (
        result,
        d_input,
        last[:own_n, :head],
        last[own_n : own_n + part],
        last[:own_n, head:].T,
        g_gate,
        g_up,
        g_down,
        gain_sums[:part],
        gain_sums[part : 2 * part],
        gain_sums[2 * part : 3 * part],
        gain_sums[3 * part : 4 * part],
        gain_sums[tail : tail + head_part],
        gain_sums[tail + head_part :],
    )


def solution(mesh):
    in_specs = (
        P("dp", "seq", None),
        P("dp", "seq"),
        P("dp", "seq", None),
        P(("dp", "seq"), "tensor"),
        P(("dp", "seq", "tensor"), None),
        P("tensor", ("dp", "seq")),
        P(("dp", "seq"), "tensor"),
        P(("dp", "seq"), "tensor"),
        P("tensor", ("dp", "seq")),
        P(("dp", "seq", "tensor")),
        P(("dp", "seq", "tensor")),
        P(("dp", "seq", "tensor")),
        P(("dp", "seq", "tensor")),
        P(("dp", "seq", "tensor")),
        P(("dp", "seq", "tensor")),
    )
    out_specs = (
        P("dp", "seq", None),
        P("dp", "seq", None),
        P(("dp", "seq"), "tensor"),
        P(("dp", "seq", "tensor"), None),
        P("tensor", ("dp", "seq")),
        P(("dp", "seq"), "tensor"),
        P(("dp", "seq"), "tensor"),
        P("tensor", ("dp", "seq")),
        P(("dp", "seq", "tensor")),
        P(("dp", "seq", "tensor")),
        P(("dp", "seq", "tensor")),
        P(("dp", "seq", "tensor")),
        P(("dp", "seq", "tensor")),
        P(("dp", "seq", "tensor")),
    )
    return jax.shard_map(body, mesh=mesh, in_specs=in_specs, out_specs=out_specs, check_vma=False)
```

```python
import jax
import jax.numpy as jnp
from jax import lax
from jax.sharding import PartitionSpec as P

EPS = 1e-06
QSCALE = 0.0625
MASKED = -1e30
LOW = jnp.bfloat16
F32 = jnp.float32
ALL = ("dp", "seq", "tensor")


def normalize(values):
    factor = lax.rsqrt(jnp.mean(values * values, axis=-1, keepdims=True) + EPS)
    return (values * factor, factor)


def norm_back(scaled, factor, upstream):
    return factor * (upstream - scaled * jnp.mean(upstream * scaled, axis=-1, keepdims=True))


def angles(positions, width_n):
    half_w = width_n // 2
    freq_t = 1000000.0 ** (-(jnp.arange(half_w, dtype=F32) * 2.0 / width_n))
    turn_t = positions.astype(F32)[..., None] * freq_t
    return (jnp.cos(turn_t), jnp.sin(turn_t))


def rotate(values, cos_t, sin_t):
    half_w = values.shape[-1] // 2
    low_v, high_v = values[..., :half_w], values[..., half_w:]
    return jnp.concatenate(
        [low_v * cos_t - high_v * sin_t, high_v * cos_t + low_v * sin_t], axis=-1
    )


def rotate_back(values, cos_t, sin_t):
    half_w = values.shape[-1] // 2
    low_v, high_v = values[..., :half_w], values[..., half_w:]
    return jnp.concatenate(
        [low_v * cos_t + high_v * sin_t, high_v * cos_t - low_v * sin_t], axis=-1
    )


def product(pattern, left_m, right_m):
    return jnp.einsum(pattern, left_m, right_m, preferred_element_type=F32)


def gelu_mix(gate_v, upper_v):
    return jax.nn.gelu(gate_v, approximate=True) * upper_v


def swap(values):
    return lax.ppermute(values, "seq", [(0, 1), (1, 0)])


def in_order(mine, theirs, axis):
    first = lax.axis_index("seq") == 0
    return jnp.stack(
        [jnp.where(first, mine, theirs), jnp.where(first, theirs, mine)], axis=axis
    )


def gather_rows(shard):
    seq_n = lax.axis_size("seq")
    if seq_n != 2:
        return lax.all_gather(shard, ("dp", "seq"), axis=0, tiled=True)
    mine = lax.all_gather(shard, "dp", axis=0, tiled=False)
    both = in_order(mine, swap(mine), 1)
    return both.reshape(-1, shard.shape[-1])


def add_dp(pair):
    dp_n = lax.axis_size("dp")
    me = lax.axis_index("dp")
    total = lax.dynamic_index_in_dim(pair, me, 0, keepdims=False).astype(F32)
    for step in range(1, dp_n):
        sent = lax.dynamic_index_in_dim(pair, lax.rem(me + step, dp_n), 0, keepdims=False)
        total = total + lax.ppermute(
            sent, "dp", [(index, (index + step) % dp_n) for index in range(dp_n)]
        ).astype(F32)
    return total


def scatter_rows(total):
    seq_n = lax.axis_size("seq")
    if seq_n != 2:
        return lax.psum_scatter(
            total, ("dp", "seq"), scatter_dimension=0, tiled=True
        ).astype(F32)
    dp_n = lax.axis_size("dp")
    me = lax.axis_index("seq")
    parts = total.reshape(dp_n, 2, -1, total.shape[-1])
    away = lax.dynamic_index_in_dim(parts, 1 - me, 1, keepdims=False)
    stay = lax.dynamic_index_in_dim(parts, me, 1, keepdims=False)
    return add_dp((stay.astype(F32) + swap(away).astype(F32)).astype(LOW))


def across(values, bit):
    return lax.ppermute(values, "tensor", [(index, index ^ bit) for index in range(4)])


def add_tensor(parts):
    if lax.axis_size("tensor") != 4:
        return lax.psum_scatter(parts, "tensor", scatter_dimension=0).astype(F32)
    me = lax.axis_index("tensor")
    low, high = lax.rem(me, 2), me // 2
    pairs = parts.reshape((2, 2) + parts.shape[1:])
    sent = lax.dynamic_index_in_dim(pairs, 1 - low, 1, keepdims=False)
    kept = lax.dynamic_index_in_dim(pairs, low, 1, keepdims=False)
    kept = (kept.astype(F32) + across(sent, 1).astype(F32)).astype(LOW)
    sent = lax.dynamic_index_in_dim(kept, 1 - high, 0, keepdims=False)
    kept = lax.dynamic_index_in_dim(kept, high, 0, keepdims=False)
    return kept.astype(F32) + across(sent, 2).astype(F32)


def sum_share(partial):
    tensor_n = lax.axis_size("tensor")
    return add_tensor(partial.astype(LOW).reshape(tensor_n, -1, partial.shape[-1]))


def spread(share):
    if lax.axis_size("tensor") != 4:
        return lax.all_gather(share, "tensor", axis=0, tiled=True)
    me = lax.axis_index("tensor")
    even, first = lax.rem(me, 2) == 0, me // 2 == 0
    other = across(share, 2)
    both = jnp.stack([jnp.where(first, share, other), jnp.where(first, other, share)], axis=0)
    other = across(both, 1)
    full = jnp.stack([jnp.where(even, both, other), jnp.where(even, other, both)], axis=1)
    return full.reshape(-1, share.shape[-1])


def gather_pack(shard):
    seq_n, dp_n = lax.axis_size("seq"), lax.axis_size("dp")
    if seq_n != 2:
        return lax.all_gather(shard, ("dp", "seq"), axis=0, tiled=False)
    me = lax.axis_index("dp")
    came = [shard]
    for step in range(1, dp_n):
        came.append(
            lax.ppermute(shard, "dp", [(index, (index + step) % dp_n) for index in range(dp_n)])
        )
    both = jnp.stack([in_order(entry, swap(entry), 0) for entry in came], axis=0)
    ordered = [
        lax.dynamic_index_in_dim(both, lax.rem(me - index + dp_n, dp_n), 0, keepdims=False)
        for index in range(dp_n)
    ]
    return jnp.concatenate(ordered, axis=0)


def add_gains(terms):
    seq_n, tensor_n = lax.axis_size("seq"), lax.axis_size("tensor")
    if seq_n != 2 or tensor_n != 4:
        return lax.psum_scatter(terms, ALL, scatter_dimension=0, tiled=True)[0]
    dp_n = lax.axis_size("dp")
    parts = terms.reshape(dp_n, 2, 4, -1)
    for bit in (1, 2):
        parts = parts + across(parts, bit)
    parts = lax.dynamic_index_in_dim(parts, lax.axis_index("tensor"), 2, keepdims=False)
    parts = parts + swap(parts)
    parts = lax.dynamic_index_in_dim(parts, lax.axis_index("seq"), 1, keepdims=False)
    return add_dp(parts)


def row_sum(values):
    return jnp.sum(values.reshape(-1, values.shape[-1]), axis=0)


def body(
    tokens,
    positions,
    out_grad,
    q_weight,
    kv_weight,
    o_weight,
    gate_weight,
    up_weight,
    down_weight,
    attn_in_gain,
    attn_out_gain,
    ffn_in_gain,
    ffn_out_gain,
    q_gain,
    k_gain,
):
    batch, local_len, width = tokens.shape
    rows_n = batch * local_len
    head = q_weight.shape[1]
    seq_n, tensor_n = lax.axis_size("seq"), lax.axis_size("tensor")
    blocks_n = lax.axis_size("dp") * seq_n
    all_n = blocks_n * tensor_n
    part = width // all_n
    head_part = head // all_n
    share_n = rows_n // tensor_n
    tensor_me = lax.axis_index("tensor")

    gain_row = jnp.concatenate(
        [attn_in_gain, attn_out_gain, ffn_in_gain, ffn_out_gain, q_gain, k_gain]
    )
    gain_n = gain_row.shape[0]
    gain_row = jnp.pad(gain_row, (0, 2 * head - gain_n))[None]
    fill = jnp.zeros((-(part + 1) % 16, 2 * head), LOW)
    small = spread(jnp.concatenate([kv_weight, gain_row, fill], axis=0))
    qo_weight = jnp.concatenate([q_weight, o_weight.T], axis=1)
    own_n = width // blocks_n
    pack = gather_pack(jnp.concatenate([qo_weight, small], axis=0))
    qo_mat = pack[:, :own_n].reshape(width, 2 * head)
    small = pack[:, own_n:].reshape(all_n, -1, 2 * head)
    kv_mat = small[:, :part].reshape(width, 2 * head)
    gains = small[:, part, :gain_n].astype(F32)

    def gain_of(index):
        return 1.0 + gains[:, index * part : (index + 1) * part].reshape(width)

    scale_ai, scale_ao, scale_fi, scale_fo = (gain_of(index) for index in range(4))
    tail = 4 * part
    scale_q = 1.0 + gains[:, tail : tail + head_part].reshape(head)
    scale_k = 1.0 + gains[:, tail + head_part :].reshape(head)

    q_mat, o_mat = qo_mat[:, :head], qo_mat[:, head:]
    gate_mat = gather_rows(gate_weight)
    up_mat = gather_rows(up_weight)
    down_mat = gather_rows(down_weight.T)

    def share(values):
        return lax.dynamic_slice_in_dim(
            values.reshape(rows_n, width), tensor_me * share_n, share_n, 0
        ).astype(F32)

    cos_t, sin_t = angles(positions, head)
    in_hat_all, unused_fac = normalize(tokens.astype(F32))
    normed = (in_hat_all * scale_ai).astype(LOW)
    kv_raw = product("scd,de->sce", normed, kv_mat)
    k_hat, k_fac = normalize(kv_raw[..., :head])
    keys_local = rotate(k_hat * scale_k, cos_t, sin_t).astype(LOW)
    both_local = jnp.concatenate([keys_local, kv_raw[..., head:].astype(LOW)], axis=-1)
    if seq_n == 2:
        key_value = in_order(both_local, swap(both_local), 1)
        key_value = key_value.reshape(batch, 2 * local_len, 2 * head)
    else:
        key_value = lax.all_gather(both_local, "seq", axis=1, tiled=True)
    key_all, value_all = key_value[..., :head], key_value[..., head:]
    q_raw = product("scd,de->sce", normed, q_mat)
    q_hat, q_fac = normalize(q_raw)
    queries = (rotate(q_hat * scale_q, cos_t, sin_t) * QSCALE).astype(LOW)
    row_ids = lax.axis_index("seq") * local_len + jnp.arange(local_len, dtype=jnp.int32)
    all_ids = jnp.arange(seq_n * local_len, dtype=jnp.int32)
    allowed = all_ids[None, :] <= row_ids[:, None]
    scores = jnp.where(allowed[None], product("sqd,skd->sqk", queries, key_all), MASKED)
    peak_v = jnp.max(scores, axis=-1, keepdims=True)
    expo_v = jnp.exp(scores - peak_v)
    probs = expo_v / jnp.sum(expo_v, axis=-1, keepdims=True)
    probs_low = probs.astype(LOW)
    attended = product("sqk,skd->sqd", probs_low, value_all).astype(LOW)
    attended_r = attended.reshape(rows_n, head)
    branch = sum_share(product("re,de->rd", attended_r, o_mat))

    inputs = share(tokens)
    in_hat, in_fac = normalize(inputs)
    back = share(out_grad)
    br_hat, br_fac = normalize(branch)
    middle = inputs + br_hat * scale_ao
    mid_hat, mid_fac = normalize(middle)
    normed_ffn = spread((mid_hat * scale_fi).astype(LOW))
    gate_v = product("rd,df->rf", normed_ffn, gate_mat)
    upper_v = product("rd,df->rf", normed_ffn, up_mat)
    acted = gelu_mix(gate_v, upper_v).astype(LOW)
    ffn_out = sum_share(product("rf,df->rd", acted, down_mat))
    ffn_hat, ffn_fac = normalize(ffn_out)
    g_fo = row_sum(back * ffn_hat)
    d_ffn = spread(norm_back(ffn_hat, ffn_fac, back * scale_fo).astype(LOW))
    result = (middle + ffn_hat * scale_fo).astype(LOW)

    g_down = product("rd,rf->df", d_ffn, acted).astype(LOW)
    d_ffn, g_down = lax.optimization_barrier((d_ffn, g_down))
    g_down = scatter_rows(g_down).T
    d_acted = product("rd,df->rf", d_ffn, down_mat)
    unused_out, pull_back = jax.vjp(gelu_mix, gate_v, upper_v)
    d_gate, d_up = pull_back(d_acted)
    d_gate = d_gate.astype(LOW)
    d_up = d_up.astype(LOW)
    d_nffn = sum_share(
        product("rf,df->rd", d_gate, gate_mat) + product("rf,df->rd", d_up, up_mat)
    )
    g_gate = product("rd,rf->df", normed_ffn, d_gate).astype(LOW)
    g_up = product("rd,rf->df", normed_ffn, d_up).astype(LOW)
    d_nffn, g_gate, g_up = lax.optimization_barrier((d_nffn, g_gate, g_up))
    g_gate = scatter_rows(g_gate)
    g_up = scatter_rows(g_up)
    g_fi = row_sum(d_nffn * mid_hat)
    d_middle = back + norm_back(mid_hat, mid_fac, d_nffn * scale_fi)
    g_ao = row_sum(d_middle * br_hat)
    d_branch = spread(norm_back(br_hat, br_fac, d_middle * scale_ao).astype(LOW))

    g_out = product("rd,re->de", d_branch, attended_r)
    d_att = product("rd,de->re", d_branch, o_mat).astype(LOW).reshape(attended.shape)
    d_att, result = lax.optimization_barrier((d_att, result))
    result = spread(result).reshape(tokens.shape)
    d_probs = product("sqd,skd->sqk", d_att, value_all)
    row_dot = jnp.sum(probs * d_probs, axis=-1, keepdims=True)
    d_scores = (probs * (d_probs - row_dot)).astype(LOW)
    key_terms = product("sqk,sqd->skd", d_scores, queries)
    value_terms = product("sqk,sqd->skd", probs_low, d_att)
    kv_terms = jnp.concatenate([key_terms, value_terms], axis=-1).astype(LOW)
    if seq_n == 2:
        me = lax.axis_index("seq")
        halves = kv_terms.reshape(batch, 2, local_len, 2 * head)
        away = lax.dynamic_index_in_dim(halves, 1 - me, 1, keepdims=False)
        stay = lax.dynamic_index_in_dim(halves, me, 1, keepdims=False)
        d_kv = stay.astype(F32) + swap(away).astype(F32)
    else:
        d_kv = lax.psum_scatter(kv_terms, "seq", scatter_dimension=1, tiled=True).astype(F32)
    d_queries = product("sqk,skd->sqd", d_scores, key_all)
    dq_turn = rotate_back(d_queries * QSCALE, cos_t, sin_t)
    g_q = row_sum(dq_turn * q_hat)
    d_qraw = norm_back(q_hat, q_fac, dq_turn * scale_q).astype(LOW)
    dk_turn = rotate_back(d_kv[..., :head], cos_t, sin_t)
    g_k = row_sum(dk_turn * k_hat)
    d_kvraw = jnp.concatenate(
        [norm_back(k_hat, k_fac, dk_turn * scale_k), d_kv[..., head:]], axis=-1
    ).astype(LOW)
    d_normed = product("sce,de->scd", d_qraw, q_mat) + product("sce,de->scd", d_kvraw, kv_mat)
    d_normed = sum_share(d_normed.reshape(rows_n, width))
    g_kv = product("scd,sce->de", normed, d_kvraw).astype(LOW)
    g_kv = g_kv.reshape(blocks_n, tensor_n, part, 2 * head)
    g_kv = add_tensor(jnp.swapaxes(g_kv, 0, 1).reshape(tensor_n, -1, 2 * head))
    g_kv = g_kv.astype(LOW).reshape(blocks_n, part, 2 * head)
    g_qmat = product("scd,sce->de", normed, d_qraw)
    g_qo = jnp.concatenate([g_qmat, g_out], axis=1).astype(LOW)
    g_qo = g_qo.reshape(blocks_n, width // blocks_n, 2 * head)
    fill = jnp.zeros((blocks_n, -(width // blocks_n + part) % 16, 2 * head), LOW)
    last = jnp.concatenate([g_qo, g_kv, fill], axis=1).reshape(-1, 2 * head)
    last = scatter_rows(last)
    g_ai = row_sum(d_normed * in_hat)
    d_input = d_middle + norm_back(in_hat, in_fac, d_normed * scale_ai)
    d_input = spread(d_input.astype(LOW)).reshape(tokens.shape)
    gain_terms = jnp.concatenate(
        [entry.reshape(all_n, -1) for entry in (g_ai, g_ao, g_fi, g_fo, g_q, g_k)], axis=1
    )
    gain_sums = add_gains(gain_terms)
    return (
        result,
        d_input,
        last[:own_n, :head],
        last[own_n : own_n + part],
        last[:own_n, head:].T,
        g_gate,
        g_up,
        g_down,
        gain_sums[:part],
        gain_sums[part : 2 * part],
        gain_sums[2 * part : 3 * part],
        gain_sums[3 * part : 4 * part],
        gain_sums[tail : tail + head_part],
        gain_sums[tail + head_part :],
    )


def solution(mesh):
    in_specs = (
        P("dp", "seq", None),
        P("dp", "seq"),
        P("dp", "seq", None),
        P(("dp", "seq"), "tensor"),
        P(("dp", "seq", "tensor"), None),
        P("tensor", ("dp", "seq")),
        P(("dp", "seq"), "tensor"),
        P(("dp", "seq"), "tensor"),
        P("tensor", ("dp", "seq")),
        P(("dp", "seq", "tensor")),
        P(("dp", "seq", "tensor")),
        P(("dp", "seq", "tensor")),
        P(("dp", "seq", "tensor")),
        P(("dp", "seq", "tensor")),
        P(("dp", "seq", "tensor")),
    )
    out_specs = (
        P("dp", "seq", None),
        P("dp", "seq", None),
        P(("dp", "seq"), "tensor"),
        P(("dp", "seq", "tensor"), None),
        P("tensor", ("dp", "seq")),
        P(("dp", "seq"), "tensor"),
        P(("dp", "seq"), "tensor"),
        P("tensor", ("dp", "seq")),
        P(("dp", "seq", "tensor")),
        P(("dp", "seq", "tensor")),
        P(("dp", "seq", "tensor")),
        P(("dp", "seq", "tensor")),
        P(("dp", "seq", "tensor")),
        P(("dp", "seq", "tensor")),
    )
    return jax.shard_map(body, mesh=mesh, in_specs=in_specs, out_specs=out_specs, check_vma=False)
```
